256 devices in a mesh: row: 8 (over y, x_hi), col: 32 (over z, x_lo, core).
Axes of the slice: x: 4 (x_hi: 2, x_lo: 2; x = x_hi * 2 + x_lo), y: 4, z: 8, core: 2. Of those that a mesh axis runs over, the one named last changes fastest.
Arguments:
- cells: bfloat16 [2, 512, 512, 256], P(None, 'row', 'col'), may hold values from -6 to 6
- w_row_qkv: bfloat16 [256, 768], replicated, may hold values from -0.375 to 0.375
- w_row_out: bfloat16 [256, 256], replicated, may hold values from -0.375 to 0.375
- w_col_qkv: bfloat16 [256, 768], replicated, may hold values from -0.375 to 0.375
- w_col_out: bfloat16 [256, 256], replicated, may hold values from -0.375 to 0.375
- w_up: bfloat16 [256, 1024], replicated, may hold values from -0.375 to 0.375
- w_down: bfloat16 [1024, 256], replicated, may hold values from -0.1875 to 0.1875
Outputs:
- updated: bfloat16 [2, 512, 512, 256], P(None, 'row', 'col')
The draws below stay inside these ranges and needn't reach their ends.
All inputs are finite; a program needn't handle non-finite values.
Results may differ from the reference program's by a relative error of at most 0.009.
Values may be sent and summed in bfloat16 or wider, within the bound.
A program may use at most 64 MiB of HBM per device.

```python
import jax
import jax.numpy as jnp
from jax import lax

MAPS = 2
H = 512
W = 512
C = 256
HEADS = 8
FF = 1024


def block_levels(rng, extent, cuts, smallest, high):
    level, own = 1.0, jax.random.fold_in(rng, 6)
    for position, shards_of in cuts:
        steps = jnp.exp(jax.random.uniform(jax.random.fold_in(own, position), (shards_of,), jnp.float32, smallest / len(cuts), high / len(cuts)))
        level = level * jnp.repeat(steps, extent[position] // shards_of).reshape([-1 if axis == position else 1 for axis in range(len(extent))])
    return level


def gaussian(key, extent, spread, limit, pieces=(), kind=jnp.bfloat16):
    factor_of = block_levels(key, extent, pieces, -0.22, 0.18) if pieces else 1.0
    drawn = jax.random.normal(key, extent, jnp.float32) * spread * factor_of
    return jnp.minimum(jnp.maximum(drawn, -limit), limit).astype(kind)


def setup_inputs(seed: int = 0) -> dict:
    splits = jax.random.split(jax.random.key(seed), 8)
    return {
        "cells": gaussian(splits[0], (MAPS, H, W, C), 1.0, 6.0, ((1, 8), (2, 32))),
        "w_row_qkv": gaussian(splits[1], (C, 3 * C), C ** -0.5, 0.375),
        "w_row_out": gaussian(splits[2], (C, C), C ** -0.5, 0.375),
        "w_col_qkv": gaussian(splits[3], (C, 3 * C), C ** -0.5, 0.375),
        "w_col_out": gaussian(splits[4], (C, C), C ** -0.5, 0.375),
        "w_up": gaussian(splits[5], (C, FF), C ** -0.5, 0.375),
        "w_down": gaussian(splits[6], (FF, C), FF ** -0.5, 0.1875),
    }


eps = 1e-06

def rms(v32):
    return v32 * lax.rsqrt(lax.optimization_barrier(jnp.mean(v32 * v32, axis=-1, keepdims=True)) + eps)

def project(seq, w_qkv):
    width = seq.shape[-1]
    normed = rms(seq.astype(jnp.float32)).astype(jnp.bfloat16)
    mixed = jnp.dot(normed, w_qkv, preferred_element_type=jnp.float32)
    query = rms(mixed[..., :width]).astype(jnp.bfloat16)
    keys = rms(mixed[..., width:2 * width]).astype(jnp.bfloat16)
    values = mixed[..., 2 * width:].astype(jnp.bfloat16)
    return (query, keys, values)

def one_sequence(triple):
    query, keys, values = triple
    length, width = query.shape
    size = width // HEADS
    q3 = query.reshape(length, HEADS, size).astype(jnp.float32)
    k3 = keys.reshape(length, HEADS, size).astype(jnp.float32)
    v3 = values.reshape(length, HEADS, size).astype(jnp.float32)
    scores = jnp.einsum('lgd,mgd->glm', q3, k3) * size ** (-0.5)
    probs = jnp.exp(scores)
    total = lax.optimization_barrier(jnp.sum(probs, axis=-1))
    weights = probs.astype(jnp.bfloat16).astype(jnp.float32)
    summed = jnp.einsum('glm,mgd->lgd', weights, v3)
    attended = summed / jnp.transpose(total)[:, :, None]
    return attended.reshape(length, width).astype(jnp.bfloat16)

def attend(seq, w_qkv, w_out):
    query, keys, values = project(seq, w_qkv)
    attended = lax.map(one_sequence, (query, keys, values))
    out = jnp.dot(attended, w_out, preferred_element_type=jnp.float32)
    return (seq.astype(jnp.float32) + out).astype(jnp.bfloat16)

def reference(cells, w_row_qkv, w_row_out, w_col_qkv, w_col_out, w_up, w_down):
    maps, rows, cols, width = cells.shape
    after_rows = attend(cells.reshape(maps * rows, cols, width), w_row_qkv, w_row_out)
    after_rows = after_rows.reshape(maps, rows, cols, width)
    by_cols = jnp.transpose(after_rows, (0, 2, 1, 3)).reshape(maps * cols, rows, width)
    after_cols = attend(by_cols, w_col_qkv, w_col_out).reshape(maps, cols, rows, width)
    after_cols = jnp.transpose(after_cols, (0, 2, 1, 3))
    normed = rms(after_cols.astype(jnp.float32)).astype(jnp.bfloat16)
    hidden = jax.nn.gelu(jnp.dot(normed, w_up, preferred_element_type=jnp.float32), approximate=True).astype(jnp.bfloat16)
    down = jnp.dot(hidden, w_down, preferred_element_type=jnp.float32)
    return (after_cols.astype(jnp.float32) + down).astype(jnp.bfloat16)
```

```python
import functools
import math

import jax
import jax.numpy as jnp
from jax import lax
from jax.experimental import pallas as pl
from jax.experimental.pallas import tpu as pltpu
from jax.sharding import PartitionSpec as P

MESH = pl.DeviceIdType.MESH
BF = jnp.bfloat16
F32 = jnp.float32
HEADS = 8
EPS = 1e-06


def rms(v, scale=None):
    r = lax.rsqrt(jnp.mean(v * v, axis=-1, keepdims=True) + EPS)
    return v * (r if scale is None else r * scale)


def mm(a, b):
    return jnp.dot(a, b, preferred_element_type=F32)


def mm_nt(a, b):
    return lax.dot_general(a, b, (((1,), (1,)), ((), ())), preferred_element_type=F32)


def permutation(size, low, ref):
    o = lax.broadcasted_iota(jnp.int32, (size, size), 0)
    s = lax.broadcasted_iota(jnp.int32, (size, size), 1)
    high = size // low
    hit = s == (o & (high - 1)) * low + lax.shift_right_logical(o, int(math.log2(high)))
    ref[...] = jnp.where(hit, 1.0, 0.0).astype(BF)


def kernel(
    nr, nc,
    x_hbm, wrq, wro, wcq, wco, wup, wdn,
    out_ref,
    wqkv, wo, up, down, seqs, stash, rowout, home2, home2t, colout, home3, res,
    q_s, k_s, w_s, perm_in, perm_out,
    w_sem, in_send, in_recv, z_send, z_recv, c_send, c_recv, b_send, b_recv,
):
    r = lax.axis_index("row")
    c = lax.axis_index("col")
    length, width = seqs.shape[1], seqs.shape[2]
    half = width // 2
    size = width // HEADS
    qscale = math.log2(math.e) / math.sqrt(size)

    weight_copies = [
        pltpu.make_async_copy(wrq, wqkv.at[0], w_sem.at[0]),
        pltpu.make_async_copy(wcq, wqkv.at[1], w_sem.at[1]),
        pltpu.make_async_copy(wro, wo.at[0], w_sem.at[2]),
        pltpu.make_async_copy(wco, wo.at[1], w_sem.at[3]),
        pltpu.make_async_copy(wup, up, w_sem.at[4]),
        pltpu.make_async_copy(wdn, down, w_sem.at[5]),
    ]
    for copy in weight_copies:
        copy.start()

    barrier = pltpu.get_barrier_semaphore()

    def greet_col(k, _):
        pl.semaphore_signal(
            barrier, inc=1, device_id={"col": lax.rem(c + k, nc)}, device_id_type=MESH
        )
        return 0

    def greet_row(k, _):
        pl.semaphore_signal(
            barrier, inc=1, device_id={"row": lax.rem(r + k, nr)}, device_id_type=MESH
        )
        return 0

    lax.fori_loop(1, nc, greet_col, 0)
    lax.fori_loop(1, nr, greet_row, 0)
    permutation(256, 8, perm_in)
    permutation(256, 16, perm_out)
    pl.semaphore_wait(barrier, nc + nr - 2)

    def tile(base, n):
        return pl.ds(pl.multiple_of(base, n), n)

    def send_in(s, _):
        m, i = lax.shift_right_logical(s, 1), s & 1

        def one(k, _):
            peer = lax.rem(c + k, nc)
            pltpu.make_async_remote_copy(
                src_ref=x_hbm.at[m, 2 * peer + i],
                dst_ref=seqs.at[s, tile(c * 16, 16)],
                send_sem=in_send.at[s],
                recv_sem=in_recv.at[s],
                device_id={"col": peer},
                device_id_type=MESH,
            ).start()
            return 0

        pltpu.make_async_copy(
            x_hbm.at[m, 2 * c + i], seqs.at[s, tile(c * 16, 16)], in_recv.at[s]
        ).start()
        lax.fori_loop(1, nc, one, 0)
        return 0

    lax.fori_loop(0, 4, send_in, 0)

    def send_back(q):
        def one(k, _):
            peer = lax.rem(c + k, nc)
            pltpu.make_async_remote_copy(
                src_ref=rowout.at[q, peer],
                dst_ref=home2.at[q, tile(c * 16, 16)],
                send_sem=z_send.at[q],
                recv_sem=z_recv.at[q],
                device_id={"col": peer},
                device_id_type=MESH,
            ).start()
            return 0

        pltpu.make_async_copy(rowout.at[q, c], home2.at[q, tile(c * 16, 16)], z_recv.at[q]).start()
        lax.fori_loop(1, nc, one, 0)

    def turn(q):
        pltpu.make_async_copy(home2.at[q], home2.at[q], z_recv.at[q]).wait()
        for b in range(2):
            moved = mm(perm_in[...], home2[q, b * 256 : (b + 1) * 256, :])
            home2t[q, :, b * 32 : (b + 1) * 32, :] = moved.reshape(8, 32, width).astype(BF)

        def one(k, _):
            peer = lax.rem(r + k, nr)
            pltpu.make_async_remote_copy(
                src_ref=home2t.at[q, peer],
                dst_ref=seqs.at[4 + q, tile(r * 64, 64)],
                send_sem=c_send.at[q],
                recv_sem=c_recv.at[q],
                device_id={"row": peer},
                device_id_type=MESH,
            ).start()
            return 0

        pltpu.make_async_copy(
            home2t.at[q, r], seqs.at[4 + q, tile(r * 64, 64)], c_recv.at[q]
        ).start()
        lax.fori_loop(1, nr, one, 0)

    def send_home(q):
        def one(k, _):
            peer = lax.rem(r + k, nr)
            pltpu.make_async_remote_copy(
                src_ref=colout.at[q, tile(peer * 64, 64)],
                dst_ref=home3.at[q, tile(r * 64, 64)],
                send_sem=b_send.at[q],
                recv_sem=b_recv.at[q],
                device_id={"row": peer},
                device_id_type=MESH,
            ).start()
            return 0

        pltpu.make_async_copy(
            colout.at[q, tile(r * 64, 64)], home3.at[q, tile(r * 64, 64)], b_recv.at[q]
        ).start()
        lax.fori_loop(1, nr, one, 0)

    lane_head = lax.shift_right_logical(
        lax.broadcasted_iota(jnp.int32, (1, width), 1), int(math.log2(size))
    )
    zero, one_ = jnp.zeros((), BF), jnp.ones((), BF)

    def attention(t):
        which = lax.shift_right_logical(t, 2)
        for b in range(0, length, 256):
            normed = rms(seqs[t, b : b + 256, :].astype(F32)).astype(BF)
            mixed = mm(normed, wqkv[which])
            q_s[b : b + 256, :] = rms(mixed[:, :width], qscale).astype(BF)
            k_s[b : b + 256, :] = rms(mixed[:, width : 2 * width]).astype(BF)
            values = mixed[:, 2 * width :].astype(BF)
            for h in range(HEADS):
                ones = jnp.where(lane_head == (h + 4) % 8, one_, zero)
                w_s[h * length + b : h * length + b + 256, :] = jnp.where(
                    lane_head == h, values, ones
                )
        queries, keys = q_s[...], k_s[...]
        sums = []
        for g in range(2):
            weights = []
            for h in range(4 * g, 4 * g + 4):
                scores = mm_nt(jnp.where(lane_head == h, queries, zero), keys)
                weights.append(jnp.exp2(scores).astype(BF))
            sums.append(
                mm(
                    jnp.concatenate(weights, axis=1),
                    w_s[4 * g * length : 4 * (g + 1) * length, :],
                )
            )
        attended = jnp.concatenate(
            [
                sums[0][:, :half] / sums[0][:, half:],
                sums[1][:, half:] / sums[1][:, :half],
            ],
            axis=1,
        ).astype(BF)
        return seqs[t].astype(F32) + mm(attended, wo[which])

    def feed_forward(q):
        pltpu.make_async_copy(home3.at[q], home3.at[q], b_recv.at[q]).wait()
        for b in range(0, length, 256):
            y = home3[q, b : b + 256, :].astype(F32)
            hidden = jax.nn.gelu(mm(rms(y).astype(BF), up[...]), approximate=True)
            res[q, b : b + 256, :] = (y + mm(hidden.astype(BF), down[...])).astype(BF)

    def finish(m):
        for b in range(4):
            parts = [
                res[2 * m + j, n * 64 + b * 16 : n * 64 + b * 16 + 16, :]
                for j in range(2)
                for n in range(8)
            ]
            moved = mm(perm_out[...], jnp.concatenate(parts, axis=0))
            out_ref[m, b * 16 : (b + 1) * 16] = moved.reshape(16, 16, width).astype(BF)

    weight_copies_done = [False]
    for copy in weight_copies:
        copy.wait()

    def step(t, _):
        @pl.when(t < 4)
        def _():
            pltpu.make_async_copy(seqs.at[t], seqs.at[t], in_recv.at[t & 3]).wait()

        @pl.when(t >= 4)
        def _():
            pltpu.make_async_copy(seqs.at[t], seqs.at[t], c_recv.at[t & 3]).wait()

        done = attention(t)

        @pl.when((t < 4) & ((t & 1) == 0))
        def _():
            stash[...] = done

        @pl.when((t < 4) & ((t & 1) == 1))
        def _():
            q = t - 1
            first = stash[...].reshape(32, 2, 8, width)
            second = done.reshape(32, 2, 8, width)
            for j in range(2):
                both = jnp.concatenate([first[:, j], second[:, j]], axis=1)
                rowout[q + j] = both.astype(BF)
            send_back(q)
            send_back(q + 1)

        @pl.when(t == 3)
        def _():
            turn(0)
            turn(1)

        @pl.when(t >= 4)
        def _():
            colout[t - 4] = done.astype(BF)
            send_home(t - 4)

        @pl.when(t == 5)
        def _():
            feed_forward(0)
            feed_forward(1)
            finish(0)
            turn(2)
            turn(3)

        return 0

    lax.fori_loop(0, 8, step, 0)
    feed_forward(2)
    feed_forward(3)
    finish(1)

    def drain(q, _):
        for ref, sem, rows in (
            (seqs, in_send, (nc - 1) * 16),
            (home2, z_send, (nc - 1) * 16),
            (colout, c_send, (nr - 1) * 64),
            (home3, b_send, (nr - 1) * 64),
        ):
            view = ref.at[q, pl.ds(0, rows)]
            pltpu.make_async_copy(view, view, sem.at[q]).wait()
        return 0

    lax.fori_loop(0, 4, drain, 0)


def solution(mesh):
    nr, nc = mesh.shape["row"], mesh.shape["col"]

    def body(cells, *weights):
        width = cells.shape[-1]
        ff = weights[4].shape[1]
        dma4 = pltpu.SemaphoreType.DMA((4,))
        return pl.pallas_call(
            functools.partial(kernel, nr, nc),
            out_shape=jax.ShapeDtypeStruct(cells.shape, BF),
            in_specs=[pl.BlockSpec(memory_space=pl.ANY)] * 7,
            out_specs=pl.BlockSpec(memory_space=pltpu.VMEM),
            scratch_shapes=[
                pltpu.VMEM((2, width, 3 * width), BF),
                pltpu.VMEM((2, width, width), BF),
                pltpu.VMEM((width, ff), BF),
                pltpu.VMEM((ff, width), BF),
                pltpu.VMEM((8, 512, width), BF),
                pltpu.VMEM((512, width), F32),
                pltpu.VMEM((4, 32, 16, width), BF),
                pltpu.VMEM((4, 512, width), BF),
                pltpu.VMEM((4, 8, 64, width), BF),
                pltpu.VMEM((4, 512, width), BF),
                pltpu.VMEM((4, 512, width), BF),
                pltpu.VMEM((4, 512, width), BF),
                pltpu.VMEM((512, width), BF),
                pltpu.VMEM((512, width), BF),
                pltpu.VMEM((HEADS * 512, width), BF),
                pltpu.VMEM((256, 256), BF),
                pltpu.VMEM((256, 256), BF),
                pltpu.SemaphoreType.DMA((6,)),
            ]
            + [dma4] * 8,
            compiler_params=pltpu.CompilerParams(
                collective_id=0, has_side_effects=True, vmem_limit_bytes=56 << 20
            ),
            name="axial",
        )(cells, *weights)

    return jax.shard_map(
        body,
        mesh=mesh,
        in_specs=(P(None, "row", "col", None),) + (P(),) * 6,
        out_specs=P(None, "row", "col", None),
        check_vma=False,
    )
```

```python
import functools
import math

import jax
import jax.numpy as jnp
from jax import lax
from jax.experimental import pallas as pl
from jax.experimental.pallas import tpu as pltpu
from jax.sharding import PartitionSpec as P

MESH = pl.DeviceIdType.MESH
BF = jnp.bfloat16
F32 = jnp.float32
HEADS = 8
EPS = 1e-06


def rms(v, scale=None):
    r = lax.rsqrt(jnp.mean(v * v, axis=-1, keepdims=True) + EPS)
    return v * (r if scale is None else r * scale)


def mm(a, b):
    return jnp.dot(a, b, preferred_element_type=F32)


def mm_nt(a, b):
    return lax.dot_general(a, b, (((1,), (1,)), ((), ())), preferred_element_type=F32)


def permutation(ref, source):
    o = lax.broadcasted_iota(jnp.int32, ref.shape, 0)
    s = lax.broadcasted_iota(jnp.int32, ref.shape, 1)
    ref[...] = jnp.where(s == source(o), 1.0, 0.0).astype(BF)


def shr(v, n):
    return lax.shift_right_logical(v, n)


def kernel(
    nr, nc, nz,
    x_hbm, wrq, wro, wcq, wco, wup, wdn,
    out_ref,
    wqkv, wo, up, down, seqs, stash, rowout, home2, home2t, colout, home3, res,
    q_s, k_s, w_s, perm_in, perm_out,
    w_sem, in_send, in_recv, z_send, z_recv, c_send, c_recv, b_send, b_recv,
):
    r = lax.axis_index("row")
    c = lax.axis_index("col")
    z, corner = shr(c, 2), c & 3
    place = r * 4 + corner

    def in_plane(other):
        return {"row": shr(other, 2), "col": z * 4 + (other & 3)}

    length, width = seqs.shape[1], seqs.shape[2]
    half = width // 2
    size = width // HEADS
    qscale = math.log2(math.e) / math.sqrt(size)

    weight_copies = [
        pltpu.make_async_copy(wrq, wqkv.at[0], w_sem.at[0]),
        pltpu.make_async_copy(wcq, wqkv.at[1], w_sem.at[1]),
        pltpu.make_async_copy(wro, wo.at[0], w_sem.at[2]),
        pltpu.make_async_copy(wco, wo.at[1], w_sem.at[3]),
        pltpu.make_async_copy(wup, up, w_sem.at[4]),
        pltpu.make_async_copy(wdn, down, w_sem.at[5]),
    ]
    for copy in weight_copies:
        copy.start()

    barrier = pltpu.get_barrier_semaphore()

    def greet_col(k, _):
        pl.semaphore_signal(
            barrier, inc=1, device_id={"col": lax.rem(c + k, nc)}, device_id_type=MESH
        )
        return 0

    def greet_plane(k, _):
        other = lax.rem(place + k, 4 * nr)
        pl.semaphore_signal(
            barrier, inc=1, device_id=in_plane(other), device_id_type=MESH
        )
        return 0

    lax.fori_loop(1, nc, greet_col, 0)
    lax.fori_loop(1, 4 * nr, greet_plane, 0)
    permutation(perm_in, lambda o: (shr(o, 4) & 1) * 128 + (o & 15) * 8 + shr(o, 5))
    permutation(perm_out, lambda o: (o & 15) * 16 + shr(o, 4))
    pl.semaphore_wait(barrier, nc - 1 + 4 * nr - 1)

    def tile(base, n):
        return pl.ds(pl.multiple_of(base, n), n)

    def send_in(s, _):
        m, i = shr(s, 1), s & 1

        def one(k, _):
            peer = lax.rem(c + k, nc)
            pltpu.make_async_remote_copy(
                src_ref=x_hbm.at[m, 2 * peer + i],
                dst_ref=seqs.at[s, tile(c * 16, 16)],
                send_sem=in_send.at[s],
                recv_sem=in_recv.at[s],
                device_id={"col": peer},
                device_id_type=MESH,
            ).start()
            return 0

        pltpu.make_async_copy(
            x_hbm.at[m, 2 * c + i], seqs.at[s, tile(c * 16, 16)], in_recv.at[s]
        ).start()
        lax.fori_loop(1, nc, one, 0)
        return 0

    lax.fori_loop(0, 4, send_in, 0)

    def send_back(q):
        def one(k, _):
            there = lax.rem(z + k, nz)
            pltpu.make_async_remote_copy(
                src_ref=rowout.at[q, there],
                dst_ref=home2.at[q, z],
                send_sem=z_send.at[q],
                recv_sem=z_recv.at[q],
                device_id={"col": there * 4 + corner},
                device_id_type=MESH,
            ).start()
            return 0

        pltpu.make_async_copy(rowout.at[q, z], home2.at[q, z], z_recv.at[q]).start()
        lax.fori_loop(1, nz, one, 0)

    def turn(q):
        pltpu.make_async_copy(home2.at[q], home2.at[q], z_recv.at[q]).wait()
        for b in range(2):
            tiles = [home2[q, n, 2 * b + p] for p in range(2) for n in range(nz)]
            moved = mm(perm_in[...], jnp.concatenate(tiles, axis=0))
            moved = moved.reshape(8, 2, 16, width).astype(BF)
            for n in range(8):
                home2t[q, 4 * n + 2 * b : 4 * n + 2 * b + 2] = moved[n]

        def one(k, _):
            other = lax.rem(place + k, 4 * nr)
            pltpu.make_async_remote_copy(
                src_ref=home2t.at[q, other],
                dst_ref=seqs.at[4 + q, tile(place * 16, 16)],
                send_sem=c_send.at[q],
                recv_sem=c_recv.at[q],
                device_id=in_plane(other),
                device_id_type=MESH,
            ).start()
            return 0

        pltpu.make_async_copy(
            home2t.at[q, place], seqs.at[4 + q, tile(place * 16, 16)], c_recv.at[q]
        ).start()
        lax.fori_loop(1, 4 * nr, one, 0)

    def send_home(q):
        def one(k, _):
            peer = lax.rem(r + k, nr)
            pltpu.make_async_remote_copy(
                src_ref=colout.at[q, tile(peer * 64, 64)],
                dst_ref=home3.at[q, tile(r * 64, 64)],
                send_sem=b_send.at[q],
                recv_sem=b_recv.at[q],
                device_id={"row": peer},
                device_id_type=MESH,
            ).start()
            return 0

        pltpu.make_async_copy(
            colout.at[q, tile(r * 64, 64)], home3.at[q, tile(r * 64, 64)], b_recv.at[q]
        ).start()
        lax.fori_loop(1, nr, one, 0)

    lane_head = shr(
        lax.broadcasted_iota(jnp.int32, (1, width), 1), int(math.log2(size))
    )
    zero, one_ = jnp.zeros((), BF), jnp.ones((), BF)

    def attention(t):
        which = shr(t, 2)
        for b in range(0, length, 256):
            normed = rms(seqs[t, b : b + 256, :].astype(F32)).astype(BF)
            mixed = mm(normed, wqkv[which])
            q_s[b : b + 256, :] = rms(mixed[:, :width], qscale).astype(BF)
            k_s[b : b + 256, :] = rms(mixed[:, width : 2 * width]).astype(BF)
            values = mixed[:, 2 * width :].astype(BF)
            for h in range(HEADS):
                ones = jnp.where(lane_head == (h + 4) % 8, one_, zero)
                w_s[h * length + b : h * length + b + 256, :] = jnp.where(
                    lane_head == h, values, ones
                )
        queries, keys = q_s[...], k_s[...]
        sums = []
        for g in range(2):
            weights = []
            for h in range(4 * g, 4 * g + 4):
                scores = mm_nt(jnp.where(lane_head == h, queries, zero), keys)
                weights.append(jnp.exp2(scores).astype(BF))
            sums.append(
                mm(
                    jnp.concatenate(weights, axis=1),
                    w_s[4 * g * length : 4 * (g + 1) * length, :],
                )
            )
        attended = jnp.concatenate(
            [
                sums[0][:, :half] / sums[0][:, half:],
                sums[1][:, half:] / sums[1][:, :half],
            ],
            axis=1,
        ).astype(BF)
        return seqs[t].astype(F32) + mm(attended, wo[which])

    def feed_forward(q):
        pltpu.make_async_copy(home3.at[q], home3.at[q], b_recv.at[q]).wait()
        for b in range(0, length, 256):
            y = home3[q, b : b + 256, :].astype(F32)
            hidden = jax.nn.gelu(mm(rms(y).astype(BF), up[...]), approximate=True)
            res[q, b : b + 256, :] = (y + mm(hidden.astype(BF), down[...])).astype(BF)

    def finish(m):
        for b in range(4):
            parts = [
                res[2 * m + j, n * 64 + b * 16 : n * 64 + b * 16 + 16, :]
                for j in range(2)
                for n in range(8)
            ]
            moved = mm(perm_out[...], jnp.concatenate(parts, axis=0))
            moved = moved.reshape(16, 16, width).astype(BF)
            for n in range(8):
                out_ref[m, n * 8 + 2 * b : n * 8 + 2 * b + 2] = moved[2 * n : 2 * n + 2]

    weight_copies_done = [False]
    for copy in weight_copies:
        copy.wait()

    def step(t, _):
        @pl.when(t < 4)
        def _():
            pltpu.make_async_copy(seqs.at[t], seqs.at[t], in_recv.at[t & 3]).wait()

        @pl.when(t >= 4)
        def _():
            pltpu.make_async_copy(seqs.at[t], seqs.at[t], c_recv.at[t & 3]).wait()

        done = attention(t)

        @pl.when((t < 4) & ((t & 1) == 0))
        def _():
            stash[...] = done

        @pl.when((t < 4) & ((t & 1) == 1))
        def _():
            q = t - 1
            first = stash[...].reshape(32, 2, 8, width)
            second = done.reshape(32, 2, 8, width)
            for j in range(2):
                both = jnp.concatenate([first[:, j], second[:, j]], axis=1)
                rowout[q + j] = both.astype(BF).reshape(rowout.shape[1:])
            send_back(q)
            send_back(q + 1)

        @pl.when(t >= 4)
        def _():
            colout[t - 4] = done.astype(BF)
            send_home(t - 4)

        @pl.when(t == 3)
        def _():
            turn(0)
            turn(1)

        @pl.when(t == 4)
        def _():
            turn(2)

        @pl.when(t == 5)
        def _():
            turn(3)

        @pl.when(t == 6)
        def _():
            feed_forward(0)

        return 0

    lax.fori_loop(0, 8, step, 0)
    feed_forward(1)
    finish(0)
    feed_forward(2)
    feed_forward(3)
    finish(1)

    def drain(q, _):
        for ref, sem, rows in (
            (seqs, in_send, (nc - 1) * 16),
            (home2, z_send, nz - 1),
            (seqs, c_send, (4 * nr - 1) * 16),
            (home3, b_send, (nr - 1) * 64),
        ):
            view = ref.at[q, pl.ds(0, rows)]
            pltpu.make_async_copy(view, view, sem.at[q]).wait()
        return 0

    lax.fori_loop(0, 4, drain, 0)


def solution(mesh):
    nr, nc = mesh.shape["row"], mesh.shape["col"]

    def body(cells, *weights):
        width = cells.shape[-1]
        ff = weights[4].shape[1]
        dma4 = pltpu.SemaphoreType.DMA((4,))
        return pl.pallas_call(
            functools.partial(kernel, nr, nc, nc // 4),
            out_shape=jax.ShapeDtypeStruct(cells.shape, BF),
            in_specs=[pl.BlockSpec(memory_space=pl.ANY)] * 7,
            out_specs=pl.BlockSpec(memory_space=pltpu.VMEM),
            scratch_shapes=[
                pltpu.VMEM((2, width, 3 * width), BF),
                pltpu.VMEM((2, width, width), BF),
                pltpu.VMEM((width, ff), BF),
                pltpu.VMEM((ff, width), BF),
                pltpu.VMEM((8, 512, width), BF),
                pltpu.VMEM((512, width), F32),
                pltpu.VMEM((4, nc // 4, 4, 16, width), BF),
                pltpu.VMEM((4, nc // 4, 4, 16, width), BF),
                pltpu.VMEM((4, 4 * nr, 16, width), BF),
                pltpu.VMEM((4, 512, width), BF),
                pltpu.VMEM((4, 512, width), BF),
                pltpu.VMEM((4, 512, width), BF),
                pltpu.VMEM((512, width), BF),
                pltpu.VMEM((512, width), BF),
                pltpu.VMEM((HEADS * 512, width), BF),
                pltpu.VMEM((256, 256), BF),
                pltpu.VMEM((256, 256), BF),
                pltpu.SemaphoreType.DMA((6,)),
            ]
            + [dma4] * 8,
            compiler_params=pltpu.CompilerParams(
                collective_id=0, has_side_effects=True, vmem_limit_bytes=56 << 20
            ),
            name="axial",
        )(cells, *weights)

    return jax.shard_map(
        body,
        mesh=mesh,
        in_specs=(P(None, "row", "col", None),) + (P(),) * 6,
        out_specs=P(None, "row", "col", None),
        check_vma=False,
    )
```

```python
import functools
import math

import jax
import jax.numpy as jnp
from jax import lax
from jax.experimental import pallas as pl
from jax.experimental.pallas import tpu as pltpu
from jax.sharding import PartitionSpec as P

MESH = pl.DeviceIdType.MESH
BF = jnp.bfloat16
F32 = jnp.float32
HEADS = 8
EPS = 1e-06


def rms(v, scale=None):
    r = lax.rsqrt(jnp.mean(v * v, axis=-1, keepdims=True) + EPS)
    return v * (r if scale is None else r * scale)


def mm(a, b):
    return jnp.dot(a, b, preferred_element_type=F32)


def mm_nt(a, b):
    return lax.dot_general(a, b, (((1,), (1,)), ((), ())), preferred_element_type=F32)


def permutation(ref, source):
    o = lax.broadcasted_iota(jnp.int32, ref.shape, 0)
    s = lax.broadcasted_iota(jnp.int32, ref.shape, 1)
    ref[...] = jnp.where(s == source(o), 1.0, 0.0).astype(BF)


def shr(v, n):
    return lax.shift_right_logical(v, n)


def kernel(
    nr, nc, nz,
    x_hbm, wrq, wro, wcq, wco, wup, wdn,
    out_ref,
    wqkv, wo, up, down, seqs, rowres, rowout, relay, relayed, colout, home3, res,
    q_s, k_s, w_s, perm_a, perm_b,
    w_sem, in_send, in_recv, p_send, p_recv, c_send, c_recv, b_send, b_recv,
):
    r = lax.axis_index("row")
    c = lax.axis_index("col")
    z, corner = shr(c, 2), c & 3
    place = r * 4 + corner

    def in_plane(other):
        return {"row": shr(other, 2), "col": z * 4 + (other & 3)}

    length, width = seqs.shape[1], seqs.shape[2]
    half = width // 2
    size = width // HEADS
    qscale = math.log2(math.e) / math.sqrt(size)

    weight_copies = [
        pltpu.make_async_copy(wrq, wqkv.at[0], w_sem.at[0]),
        pltpu.make_async_copy(wcq, wqkv.at[1], w_sem.at[1]),
        pltpu.make_async_copy(wro, wo.at[0], w_sem.at[2]),
        pltpu.make_async_copy(wco, wo.at[1], w_sem.at[3]),
        pltpu.make_async_copy(wup, up, w_sem.at[4]),
        pltpu.make_async_copy(wdn, down, w_sem.at[5]),
    ]
    for copy in weight_copies:
        copy.start()

    barrier = pltpu.get_barrier_semaphore()

    def greet_col(k, _):
        pl.semaphore_signal(
            barrier, inc=1, device_id={"col": lax.rem(c + k, nc)}, device_id_type=MESH
        )
        return 0

    def greet_plane(k, _):
        other = lax.rem(place + k, 4 * nr)
        pl.semaphore_signal(
            barrier, inc=1, device_id=in_plane(other), device_id_type=MESH
        )
        return 0

    lax.fori_loop(1, nc, greet_col, 0)
    lax.fori_loop(1, 4 * nr, greet_plane, 0)
    permutation(perm_a, lambda o: (o & 15) * 16 + shr(o, 4))
    permutation(perm_b, lambda o: (o & 31) * 8 + shr(o, 5))
    pl.semaphore_wait(barrier, nc - 1 + 4 * nr - 1)

    def tile(base, n):
        return pl.ds(pl.multiple_of(base, n), n)

    def send_in(s, _):
        m, i = shr(s, 1), s & 1

        def one(k, _):
            peer = lax.rem(c + nc + (1 - 2 * (k & 1)) * shr(k + 1, 1), nc)
            pltpu.make_async_remote_copy(
                src_ref=x_hbm.at[m, 2 * peer + i],
                dst_ref=seqs.at[s, tile(c * 16, 16)],
                send_sem=in_send.at[s],
                recv_sem=in_recv.at[s],
                device_id={"col": peer},
                device_id_type=MESH,
            ).start()
            return 0

        pltpu.make_async_copy(
            x_hbm.at[m, 2 * c + i], seqs.at[s, tile(c * 16, 16)], in_recv.at[s]
        ).start()
        lax.fori_loop(1, nc, one, 0)
        return 0

    lax.fori_loop(0, 4, send_in, 0)

    def split(m):
        for b in range(4):
            tiles = [
                rowres[i, n * 64 + b * 16 : n * 64 + b * 16 + 16, :]
                for i in range(2)
                for n in range(nz)
            ]
            moved = mm(perm_a[...], jnp.concatenate(tiles, axis=0))
            moved = moved.reshape(2, 8, 16, width).astype(BF)
            for j in range(2):
                for n in range(8):
                    rowout[2 * m + j, 4 * n + b] = moved[j, n]

    def across(q):
        def one(k, _):
            other = place ^ (4 * nr - k)
            pltpu.make_async_remote_copy(
                src_ref=rowout.at[q, other],
                dst_ref=relay.at[q, tile(place * 16, 16)],
                send_sem=p_send.at[q],
                recv_sem=p_recv.at[q],
                device_id=in_plane(other),
                device_id_type=MESH,
            ).start()
            return 0

        pltpu.make_async_copy(
            rowout.at[q, place], relay.at[q, tile(place * 16, 16)], p_recv.at[q]
        ).start()
        lax.fori_loop(1, 4 * nr, one, 0)

    def forward(q):
        pltpu.make_async_copy(relay.at[q], relay.at[q], p_recv.at[q]).wait()
        for b in range(2):
            moved = mm(perm_b[...], relay[q, b * 256 : (b + 1) * 256, :])
            moved = moved.reshape(nz, 32, width).astype(BF)
            relayed[q, :, b * 32 : (b + 1) * 32, :] = moved

        def one(k, _):
            there = lax.rem(z + k, nz)
            pltpu.make_async_remote_copy(
                src_ref=relayed.at[q, there],
                dst_ref=seqs.at[4 + q, tile(z * 64, 64)],
                send_sem=c_send.at[q],
                recv_sem=c_recv.at[q],
                device_id={"col": there * 4 + corner},
                device_id_type=MESH,
            ).start()
            return 0

        pltpu.make_async_copy(
            relayed.at[q, z], seqs.at[4 + q, tile(z * 64, 64)], c_recv.at[q]
        ).start()
        lax.fori_loop(1, nz, one, 0)

    def send_home(q):
        def one(k, _):
            peer = r ^ (nr - k)
            pltpu.make_async_remote_copy(
                src_ref=colout.at[q, tile(peer * 64, 64)],
                dst_ref=home3.at[q, tile(r * 64, 64)],
                send_sem=b_send.at[q],
                recv_sem=b_recv.at[q],
                device_id={"row": peer},
                device_id_type=MESH,
            ).start()
            return 0

        pltpu.make_async_copy(
            colout.at[q, tile(r * 64, 64)], home3.at[q, tile(r * 64, 64)], b_recv.at[q]
        ).start()
        lax.fori_loop(1, nr, one, 0)

    lane_head = shr(
        lax.broadcasted_iota(jnp.int32, (1, width), 1), int(math.log2(size))
    )
    zero, one_ = jnp.zeros((), BF), jnp.ones((), BF)

    def attention(t):
        which = shr(t, 2)
        for b in range(0, length, 256):
            normed = rms(seqs[t, b : b + 256, :].astype(F32)).astype(BF)
            mixed = mm(normed, wqkv[which])
            q_s[b : b + 256, :] = rms(mixed[:, :width], qscale).astype(BF)
            k_s[b : b + 256, :] = rms(mixed[:, width : 2 * width]).astype(BF)
            values = mixed[:, 2 * width :].astype(BF)
            for h in range(HEADS):
                ones = jnp.where(lane_head == (h + 4) % 8, one_, zero)
                w_s[h * length + b : h * length + b + 256, :] = jnp.where(
                    lane_head == h, values, ones
                )
        queries, keys = q_s[...], k_s[...]
        sums = []
        for g in range(2):
            weights = []
            for h in range(4 * g, 4 * g + 4):
                scores = mm_nt(jnp.where(lane_head == h, queries, zero), keys)
                weights.append(jnp.exp2(scores).astype(BF))
            sums.append(
                mm(
                    jnp.concatenate(weights, axis=1),
                    w_s[4 * g * length : 4 * (g + 1) * length, :],
                )
            )
        attended = jnp.concatenate(
            [
                sums[0][:, :half] / sums[0][:, half:],
                sums[1][:, half:] / sums[1][:, :half],
            ],
            axis=1,
        ).astype(BF)
        return seqs[t].astype(F32) + mm(attended, wo[which])

    def feed_forward(q):
        pltpu.make_async_copy(home3.at[q], home3.at[q], b_recv.at[q]).wait()
        for b in range(0, length, 256):
            y = home3[q, b : b + 256, :].astype(F32)
            hidden = jax.nn.gelu(mm(rms(y).astype(BF), up[...]), approximate=True)
            res[q, b : b + 256, :] = (y + mm(hidden.astype(BF), down[...])).astype(BF)

    def finish(m):
        for b in range(4):
            parts = [
                res[2 * m + j, n * 64 + b * 16 : n * 64 + b * 16 + 16, :]
                for j in range(2)
                for n in range(8)
            ]
            moved = mm(perm_a[...], jnp.concatenate(parts, axis=0))
            out_ref[m, b * 16 : (b + 1) * 16] = moved.reshape(16, 16, width).astype(BF)

    for copy in weight_copies:
        copy.wait()

    def step(t, _):
        @pl.when(t < 4)
        def _():
            pltpu.make_async_copy(seqs.at[t], seqs.at[t], in_recv.at[t & 3]).wait()

        @pl.when(t >= 4)
        def _():
            pltpu.make_async_copy(seqs.at[t], seqs.at[t], c_recv.at[t & 3]).wait()

        done = attention(t)

        @pl.when(t < 4)
        def _():
            rowres[t & 1] = done.astype(BF)

        @pl.when(t >= 4)
        def _():
            pieces = [
                done[n * 64 + p * 8 : n * 64 + p * 8 + 8, :] for p in range(nr) for n in range(nz)
            ]
            colout[t - 4] = jnp.concatenate(pieces, axis=0).astype(BF)
            send_home(t - 4)

        @pl.when(t == 1)
        def _():
            split(0)
            across(0)

        @pl.when(t == 2)
        def _():
            across(1)
            forward(0)

        @pl.when(t == 3)
        def _():
            split(1)
            across(2)
            forward(1)
            across(3)

        @pl.when(t == 4)
        def _():
            forward(2)

        @pl.when(t == 5)
        def _():
            forward(3)
            feed_forward(0)

        @pl.when(t == 6)
        def _():
            feed_forward(1)
            finish(0)

        return 0

    lax.fori_loop(0, 8, step, 0)
    feed_forward(2)
    feed_forward(3)
    finish(1)

    def drain(q, _):
        for ref, sem, rows in (
            (seqs, in_send, (nc - 1) * 16),
            (seqs, p_send, (4 * nr - 1) * 16),
            (seqs, c_send, (nz - 1) * 64),
            (home3, b_send, (nr - 1) * 64),
        ):
            view = ref.at[q, pl.ds(0, rows)]
            pltpu.make_async_copy(view, view, sem.at[q]).wait()
        return 0

    lax.fori_loop(0, 4, drain, 0)


def solution(mesh):
    nr, nc = mesh.shape["row"], mesh.shape["col"]

    def body(cells, *weights):
        width = cells.shape[-1]
        ff = weights[4].shape[1]
        dma4 = pltpu.SemaphoreType.DMA((4,))
        return pl.pallas_call(
            functools.partial(kernel, nr, nc, nc // 4),
            out_shape=jax.ShapeDtypeStruct(cells.shape, BF),
            in_specs=[pl.BlockSpec(memory_space=pl.ANY)] * 7,
            out_specs=pl.BlockSpec(memory_space=pltpu.VMEM),
            scratch_shapes=[
                pltpu.VMEM((2, width, 3 * width), BF),
                pltpu.VMEM((2, width, width), BF),
                pltpu.VMEM((width, ff), BF),
                pltpu.VMEM((ff, width), BF),
                pltpu.VMEM((8, 512, width), BF),
                pltpu.VMEM((2, 512, width), BF),
                pltpu.VMEM((4, 4 * nr, 16, width), BF),
                pltpu.VMEM((4, 512, width), BF),
                pltpu.VMEM((4, nc // 4, 64, width), BF),
                pltpu.VMEM((4, 512, width), BF),
                pltpu.VMEM((4, 512, width), BF),
                pltpu.VMEM((4, 512, width), BF),
                pltpu.VMEM((512, width), BF),
                pltpu.VMEM((512, width), BF),
                pltpu.VMEM((HEADS * 512, width), BF),
                pltpu.VMEM((256, 256), BF),
                pltpu.VMEM((256, 256), BF),
                pltpu.SemaphoreType.DMA((6,)),
            ]
            + [dma4] * 8,
            compiler_params=pltpu.CompilerParams(
                collective_id=0, has_side_effects=True, vmem_limit_bytes=56 << 20
            ),
            name="axial",
        )(cells, *weights)

    return jax.shard_map(
        body,
        mesh=mesh,
        in_specs=(P(None, "row", "col", None),) + (P(),) * 6,
        out_specs=P(None, "row", "col", None),
        check_vma=False,
    )
```

```python
import functools
import math

import jax
import jax.numpy as jnp
from jax import lax
from jax.experimental import pallas as pl
from jax.experimental.pallas import tpu as pltpu
from jax.sharding import PartitionSpec as P

MESH = pl.DeviceIdType.MESH
BF = jnp.bfloat16
F32 = jnp.float32
HEADS = 8
EPS = 1e-06


def rms(v, scale=None):
    r = lax.rsqrt(jnp.mean(v * v, axis=-1, keepdims=True) + EPS)
    return v * (r if scale is None else r * scale)


def mm(a, b):
    return jnp.dot(a, b, preferred_element_type=F32)


def mm_nt(a, b):
    return lax.dot_general(a, b, (((1,), (1,)), ((), ())), preferred_element_type=F32)


def permutation(ref, source):
    o = lax.broadcasted_iota(jnp.int32, ref.shape, 0)
    s = lax.broadcasted_iota(jnp.int32, ref.shape, 1)
    ref[...] = jnp.where(s == source(o), 1.0, 0.0).astype(BF)


def shr(v, n):
    return lax.shift_right_logical(v, n)


def kernel(
    nr, nc, nz,
    x_hbm, wrq, wro, wcq, wco, wup, wdn,
    out_ref,
    wqkv, wo, up, down, seqs, rowres, rowout, relay, relayed, colout, home3, res,
    q_s, k_s, w_s, perm_a, perm_b, out_v,
    w_sem, o_sem, in_send, in_recv, p_send, p_recv, c_send, c_recv, b_send, b_recv,
):
    r = lax.axis_index("row")
    c = lax.axis_index("col")
    z, corner = shr(c, 2), c & 3
    place = r * 4 + corner

    def in_plane(other):
        return {"row": shr(other, 2), "col": z * 4 + (other & 3)}

    length, width = seqs.shape[1], seqs.shape[2]
    half = width // 2
    size = width // HEADS
    qscale = math.log2(math.e) / math.sqrt(size)

    weight_copies = [
        pltpu.make_async_copy(wrq, wqkv.at[0], w_sem.at[0]),
        pltpu.make_async_copy(wcq, wqkv.at[1], w_sem.at[1]),
        pltpu.make_async_copy(wro, wo.at[0], w_sem.at[2]),
        pltpu.make_async_copy(wco, wo.at[1], w_sem.at[3]),
        pltpu.make_async_copy(wup, up, w_sem.at[4]),
        pltpu.make_async_copy(wdn, down, w_sem.at[5]),
    ]
    for copy in weight_copies:
        copy.start()

    barrier = pltpu.get_barrier_semaphore()

    def greet_col(k, _):
        pl.semaphore_signal(
            barrier, inc=1, device_id={"col": lax.rem(c + k, nc)}, device_id_type=MESH
        )
        return 0

    def greet_plane(k, _):
        other = lax.rem(place + k, 4 * nr)
        pl.semaphore_signal(
            barrier, inc=1, device_id=in_plane(other), device_id_type=MESH
        )
        return 0

    lax.fori_loop(1, nc, greet_col, 0)
    lax.fori_loop(1, 4 * nr, greet_plane, 0)
    permutation(perm_a, lambda o: (o & 15) * 16 + shr(o, 4))
    permutation(perm_b, lambda o: (o & 31) * 8 + shr(o, 5))
    pl.semaphore_wait(barrier, nc - 1 + 4 * nr - 1)

    def tile(base, n):
        return pl.ds(pl.multiple_of(base, n), n)

    def send_in(s, _):
        m, i = shr(s, 1), s & 1

        def one(k, _):
            peer = lax.rem(c + nc + (1 - 2 * (k & 1)) * shr(k + 1, 1), nc)
            pltpu.make_async_remote_copy(
                src_ref=x_hbm.at[m, 2 * peer + i],
                dst_ref=seqs.at[s, tile(c * 16, 16)],
                send_sem=in_send.at[s],
                recv_sem=in_recv.at[s],
                device_id={"col": peer},
                device_id_type=MESH,
            ).start()
            return 0

        pltpu.make_async_copy(
            x_hbm.at[m, 2 * c + i], seqs.at[s, tile(c * 16, 16)], in_recv.at[s]
        ).start()
        lax.fori_loop(1, nc, one, 0)
        return 0

    lax.fori_loop(0, 4, send_in, 0)

    def split(m):
        for b in range(4):
            tiles = [
                rowres[i, n * 64 + b * 16 : n * 64 + b * 16 + 16, :]
                for i in range(2)
                for n in range(nz)
            ]
            moved = mm(perm_a[...], jnp.concatenate(tiles, axis=0))
            moved = moved.reshape(2, 8, 16, width).astype(BF)
            for j in range(2):
                for n in range(8):
                    rowout[2 * m + j, 4 * n + b] = moved[j, n]

    def across(q):
        def one(k, _):
            other = place ^ (4 * nr - k)
            pltpu.make_async_remote_copy(
                src_ref=rowout.at[q, other],
                dst_ref=relay.at[q, tile(place * 16, 16)],
                send_sem=p_send.at[q],
                recv_sem=p_recv.at[q],
                device_id=in_plane(other),
                device_id_type=MESH,
            ).start()
            return 0

        pltpu.make_async_copy(
            rowout.at[q, place], relay.at[q, tile(place * 16, 16)], p_recv.at[q]
        ).start()
        lax.fori_loop(1, 4 * nr, one, 0)

    def forward(q):
        pltpu.make_async_copy(relay.at[q], relay.at[q], p_recv.at[q]).wait()
        for b in range(2):
            moved = mm(perm_b[...], relay[q, b * 256 : (b + 1) * 256, :])
            moved = moved.reshape(nz, 32, width).astype(BF)
            relayed[q, :, b * 32 : (b + 1) * 32, :] = moved

        def one(k, _):
            there = lax.rem(z + k, nz)
            pltpu.make_async_remote_copy(
                src_ref=relayed.at[q, there],
                dst_ref=seqs.at[4 + q, tile(z * 64, 64)],
                send_sem=c_send.at[q],
                recv_sem=c_recv.at[q],
                device_id={"col": there * 4 + corner},
                device_id_type=MESH,
            ).start()
            return 0

        pltpu.make_async_copy(
            relayed.at[q, z], seqs.at[4 + q, tile(z * 64, 64)], c_recv.at[q]
        ).start()
        lax.fori_loop(1, nz, one, 0)

    def send_home(q):
        def one(k, _):
            peer = r ^ (nr - k)
            pltpu.make_async_remote_copy(
                src_ref=colout.at[q, tile(peer * 64, 64)],
                dst_ref=home3.at[q, tile(r * 64, 64)],
                send_sem=b_send.at[q],
                recv_sem=b_recv.at[q],
                device_id={"row": peer},
                device_id_type=MESH,
            ).start()
            return 0

        pltpu.make_async_copy(
            colout.at[q, tile(r * 64, 64)], home3.at[q, tile(r * 64, 64)], b_recv.at[q]
        ).start()
        lax.fori_loop(1, nr, one, 0)

    lane_head = shr(
        lax.broadcasted_iota(jnp.int32, (1, width), 1), int(math.log2(size))
    )
    zero, one_ = jnp.zeros((), BF), jnp.ones((), BF)

    def attention(t):
        which = shr(t, 2)
        for b in range(0, length, 256):
            normed = rms(seqs[t, b : b + 256, :].astype(F32)).astype(BF)
            mixed = mm(normed, wqkv[which])
            q_s[b : b + 256, :] = rms(mixed[:, :width], qscale).astype(BF)
            k_s[b : b + 256, :] = rms(mixed[:, width : 2 * width]).astype(BF)
            values = mixed[:, 2 * width :].astype(BF)
            for h in range(HEADS):
                ones = jnp.where(lane_head == (h + 4) % 8, one_, zero)
                w_s[h * length + b : h * length + b + 256, :] = jnp.where(
                    lane_head == h, values, ones
                )
        queries, keys = q_s[...], k_s[...]
        sums = []
        for g in range(2):
            weights = []
            for h in range(4 * g, 4 * g + 4):
                scores = mm_nt(jnp.where(lane_head == h, queries, zero), keys)
                weights.append(jnp.exp2(scores).astype(BF))
            sums.append(
                mm(
                    jnp.concatenate(weights, axis=1),
                    w_s[4 * g * length : 4 * (g + 1) * length, :],
                )
            )
        attended = jnp.concatenate(
            [
                sums[0][:, :half] / sums[0][:, half:],
                sums[1][:, half:] / sums[1][:, :half],
            ],
            axis=1,
        ).astype(BF)
        return seqs[t].astype(F32) + mm(attended, wo[which])

    def feed_forward(q):
        pltpu.make_async_copy(home3.at[q], home3.at[q], b_recv.at[q]).wait()
        for b in range(0, length, 256):
            y = home3[q, b : b + 256, :].astype(F32)
            hidden = jax.nn.gelu(mm(rms(y).astype(BF), up[...]), approximate=True)
            res[q, b : b + 256, :] = (y + mm(hidden.astype(BF), down[...])).astype(BF)

    def out_copy(m, b):
        rows = pl.ds(b * 16, 16)
        return pltpu.make_async_copy(out_v.at[m, rows], out_ref.at[m, rows], o_sem.at[m, b])

    def finish(m):
        for b in range(4):
            parts = [
                res[2 * m + j, n * 64 + b * 16 : n * 64 + b * 16 + 16, :]
                for j in range(2)
                for n in range(8)
            ]
            moved = mm(perm_a[...], jnp.concatenate(parts, axis=0))
            out_v[m, b * 16 : (b + 1) * 16] = moved.reshape(16, 16, width).astype(BF)
            out_copy(m, b).start()

    for copy in weight_copies:
        copy.wait()

    def step(t, _):
        @pl.when(t < 4)
        def _():
            pltpu.make_async_copy(seqs.at[t], seqs.at[t], in_recv.at[t & 3]).wait()

        @pl.when(t >= 4)
        def _():
            pltpu.make_async_copy(seqs.at[t], seqs.at[t], c_recv.at[t & 3]).wait()

        done = attention(t)

        @pl.when(t < 4)
        def _():
            rowres[t & 1] = done.astype(BF)

        @pl.when(t >= 4)
        def _():
            pieces = [
                done[n * 64 + p * 8 : n * 64 + p * 8 + 8, :] for p in range(nr) for n in range(nz)
            ]
            colout[t - 4] = jnp.concatenate(pieces, axis=0).astype(BF)
            send_home(t - 4)

        @pl.when(t == 1)
        def _():
            split(0)
            across(0)

        @pl.when(t == 2)
        def _():
            across(1)
            forward(0)

        @pl.when(t == 3)
        def _():
            split(1)
            across(2)
            across(3)
            forward(1)
            forward(2)

        @pl.when(t == 4)
        def _():
            forward(3)

        @pl.when(t == 5)
        def _():
            feed_forward(0)

        return 0

    lax.fori_loop(0, 8, step, 0)
    feed_forward(1)
    finish(0)
    feed_forward(2)
    feed_forward(3)
    finish(1)

    def drain(q, _):
        for ref, sem, rows in (
            (seqs, in_send, (nc - 1) * 16),
            (seqs, p_send, (4 * nr - 1) * 16),
            (seqs, c_send, (nz - 1) * 64),
            (home3, b_send, (nr - 1) * 64),
        ):
            view = ref.at[q, pl.ds(0, rows)]
            pltpu.make_async_copy(view, view, sem.at[q]).wait()
        return 0

    lax.fori_loop(0, 4, drain, 0)
    for m in range(2):
        for b in range(4):
            out_copy(m, b).wait()


def solution(mesh):
    nr, nc = mesh.shape["row"], mesh.shape["col"]

    def body(cells, *weights):
        width = cells.shape[-1]
        ff = weights[4].shape[1]
        dma4 = pltpu.SemaphoreType.DMA((4,))
        return pl.pallas_call(
            functools.partial(kernel, nr, nc, nc // 4),
            out_shape=jax.ShapeDtypeStruct(cells.shape, BF),
            in_specs=[pl.BlockSpec(memory_space=pl.ANY)] * 7,
            out_specs=pl.BlockSpec(memory_space=pl.ANY),
            scratch_shapes=[
                pltpu.VMEM((2, width, 3 * width), BF),
                pltpu.VMEM((2, width, width), BF),
                pltpu.VMEM((width, ff), BF),
                pltpu.VMEM((ff, width), BF),
                pltpu.VMEM((8, 512, width), BF),
                pltpu.VMEM((2, 512, width), BF),
                pltpu.VMEM((4, 4 * nr, 16, width), BF),
                pltpu.VMEM((4, 512, width), BF),
                pltpu.VMEM((4, nc // 4, 64, width), BF),
                pltpu.VMEM((4, 512, width), BF),
                pltpu.VMEM((4, 512, width), BF),
                pltpu.VMEM((4, 512, width), BF),
                pltpu.VMEM((512, width), BF),
                pltpu.VMEM((512, width), BF),
                pltpu.VMEM((HEADS * 512, width), BF),
                pltpu.VMEM((256, 256), BF),
                pltpu.VMEM((256, 256), BF),
                pltpu.VMEM(cells.shape, BF),
                pltpu.SemaphoreType.DMA((6,)),
                pltpu.SemaphoreType.DMA((2, 4)),
            ]
            + [dma4] * 8,
            compiler_params=pltpu.CompilerParams(
                collective_id=0, has_side_effects=True, vmem_limit_bytes=56 << 20
            ),
            name="axial",
        )(cells, *weights)

    return jax.shard_map(
        body,
        mesh=mesh,
        in_specs=(P(None, "row", "col", None),) + (P(),) * 6,
        out_specs=P(None, "row", "col", None),
        check_vma=False,
    )
```

```python
import functools
import math

import jax
import jax.numpy as jnp
from jax import lax
from jax.experimental import pallas as pl
from jax.experimental.pallas import tpu as pltpu
from jax.sharding import PartitionSpec as P

MESH = pl.DeviceIdType.MESH
BF = jnp.bfloat16
F32 = jnp.float32
HEADS = 8
EPS = 1e-06


def rms(v, scale=None):
    r = lax.rsqrt(jnp.mean(v * v, axis=-1, keepdims=True) + EPS)
    return v * (r if scale is None else r * scale)


def mm(a, b):
    return jnp.dot(a, b, preferred_element_type=F32)


def mm_nt(a, b):
    return lax.dot_general(a, b, (((1,), (1,)), ((), ())), preferred_element_type=F32)


def permutation(ref, source):
    o = lax.broadcasted_iota(jnp.int32, ref.shape, 0)
    s = lax.broadcasted_iota(jnp.int32, ref.shape, 1)
    ref[...] = jnp.where(s == source(o), 1.0, 0.0).astype(BF)


def shr(v, n):
    return lax.shift_right_logical(v, n)


def kernel(
    nr, nc, nz,
    x_hbm, wrq, wro, wcq, wco, wup, wdn,
    out_ref,
    wqkv, wo, up, down, seqs, rowres, rowout, relay, relayed, colout, home3, res,
    q_s, k_s, w_s, perm_a, perm_b, out_v,
    w_sem, o_sem, in_send, in_recv, p_send, p_recv, c_send, c_recv, b_send, b_recv,
):
    r = lax.axis_index("row")
    c = lax.axis_index("col")
    z, corner = shr(c, 2), c & 3
    place = r * 4 + corner

    def in_plane(other):
        return {"row": shr(other, 2), "col": z * 4 + (other & 3)}

    length, width = seqs.shape[1], seqs.shape[2]
    half = width // 2
    size = width // HEADS
    qscale = math.log2(math.e) / math.sqrt(size)

    weight_copies = [
        pltpu.make_async_copy(wrq, wqkv.at[0], w_sem.at[0]),
        pltpu.make_async_copy(wcq, wqkv.at[1], w_sem.at[1]),
        pltpu.make_async_copy(wro, wo.at[0], w_sem.at[2]),
        pltpu.make_async_copy(wco, wo.at[1], w_sem.at[3]),
        pltpu.make_async_copy(wup, up, w_sem.at[4]),
        pltpu.make_async_copy(wdn, down, w_sem.at[5]),
    ]
    for copy in weight_copies:
        copy.start()

    barrier = pltpu.get_barrier_semaphore()

    def greet_col(k, _):
        pl.semaphore_signal(
            barrier, inc=1, device_id={"col": lax.rem(c + k, nc)}, device_id_type=MESH
        )
        return 0

    def greet_plane(k, _):
        other = lax.rem(place + k, 4 * nr)
        pl.semaphore_signal(
            barrier, inc=1, device_id=in_plane(other), device_id_type=MESH
        )
        return 0

    lax.fori_loop(1, nc, greet_col, 0)
    lax.fori_loop(1, 4 * nr, greet_plane, 0)
    permutation(perm_a, lambda o: (o & 15) * 16 + shr(o, 4))
    permutation(perm_b, lambda o: (o & 31) * 8 + shr(o, 5))
    pl.semaphore_wait(barrier, nc - 1 + 4 * nr - 1)

    def tile(base, n):
        return pl.ds(pl.multiple_of(base, n), n)

    def send_in(s, _):
        m, i = shr(s, 1), s & 1

        def one(k, _):
            peer = lax.rem(c + nc + (1 - 2 * (k & 1)) * shr(k + 1, 1), nc)
            pltpu.make_async_remote_copy(
                src_ref=x_hbm.at[m, 2 * peer + i],
                dst_ref=seqs.at[s, tile(c * 16, 16)],
                send_sem=in_send.at[s],
                recv_sem=in_recv.at[s],
                device_id={"col": peer},
                device_id_type=MESH,
            ).start()
            return 0

        pltpu.make_async_copy(
            x_hbm.at[m, 2 * c + i], seqs.at[s, tile(c * 16, 16)], in_recv.at[s]
        ).start()
        lax.fori_loop(1, nc, one, 0, unroll=True)
        return 0

    lax.fori_loop(0, 4, send_in, 0)

    def split(m):
        for b in range(4):
            tiles = [
                rowres[i, n * 64 + b * 16 : n * 64 + b * 16 + 16, :]
                for i in range(2)
                for n in range(nz)
            ]
            moved = mm(perm_a[...], jnp.concatenate(tiles, axis=0))
            moved = moved.reshape(2, 8, 16, width).astype(BF)
            for j in range(2):
                for n in range(8):
                    rowout[2 * m + j, 4 * n + b] = moved[j, n]

    def across(q):
        def one(k, _):
            other = place ^ (4 * nr - k)
            pltpu.make_async_remote_copy(
                src_ref=rowout.at[q, other],
                dst_ref=relay.at[q, tile(place * 16, 16)],
                send_sem=p_send.at[q],
                recv_sem=p_recv.at[q],
                device_id=in_plane(other),
                device_id_type=MESH,
            ).start()
            return 0

        pltpu.make_async_copy(
            rowout.at[q, place], relay.at[q, tile(place * 16, 16)], p_recv.at[q]
        ).start()
        lax.fori_loop(1, 4 * nr, one, 0, unroll=True)

    def forward(q):
        pltpu.make_async_copy(relay.at[q], relay.at[q], p_recv.at[q]).wait()
        for b in range(2):
            moved = mm(perm_b[...], relay[q, b * 256 : (b + 1) * 256, :])
            moved = moved.reshape(nz, 32, width).astype(BF)
            relayed[q, :, b * 32 : (b + 1) * 32, :] = moved

        def one(k, _):
            there = lax.rem(z + k, nz)
            pltpu.make_async_remote_copy(
                src_ref=relayed.at[q, there],
                dst_ref=seqs.at[4 + q, tile(z * 64, 64)],
                send_sem=c_send.at[q],
                recv_sem=c_recv.at[q],
                device_id={"col": there * 4 + corner},
                device_id_type=MESH,
            ).start()
            return 0

        pltpu.make_async_copy(
            relayed.at[q, z], seqs.at[4 + q, tile(z * 64, 64)], c_recv.at[q]
        ).start()
        lax.fori_loop(1, nz, one, 0)

    def send_home(q):
        def one(k, _):
            peer = r ^ (nr - k)
            pltpu.make_async_remote_copy(
                src_ref=colout.at[q, tile(peer * 64, 64)],
                dst_ref=home3.at[q, tile(r * 64, 64)],
                send_sem=b_send.at[q],
                recv_sem=b_recv.at[q],
                device_id={"row": peer},
                device_id_type=MESH,
            ).start()
            return 0

        pltpu.make_async_copy(
            colout.at[q, tile(r * 64, 64)], home3.at[q, tile(r * 64, 64)], b_recv.at[q]
        ).start()
        lax.fori_loop(1, nr, one, 0)

    lane_head = shr(
        lax.broadcasted_iota(jnp.int32, (1, width), 1), int(math.log2(size))
    )
    zero, one_ = jnp.zeros((), BF), jnp.ones((), BF)

    def attention(t):
        which = shr(t, 2)
        for b in range(0, length, 256):
            normed = rms(seqs[t, b : b + 256, :].astype(F32)).astype(BF)
            mixed = mm(normed, wqkv[which])
            q_s[b : b + 256, :] = rms(mixed[:, :width], qscale).astype(BF)
            k_s[b : b + 256, :] = rms(mixed[:, width : 2 * width]).astype(BF)
            values = mixed[:, 2 * width :].astype(BF)
            for h in range(HEADS):
                ones = jnp.where(lane_head == (h + 4) % 8, one_, zero)
                w_s[h * length + b : h * length + b + 256, :] = jnp.where(
                    lane_head == h, values, ones
                )
        queries, keys = q_s[...], k_s[...]
        sums = []
        for g in range(2):
            weights = []
            for h in range(4 * g, 4 * g + 4):
                scores = mm_nt(jnp.where(lane_head == h, queries, zero), keys)
                weights.append(jnp.exp2(scores).astype(BF))
            sums.append(
                mm(
                    jnp.concatenate(weights, axis=1),
                    w_s[4 * g * length : 4 * (g + 1) * length, :],
                )
            )
        attended = jnp.concatenate(
            [
                sums[0][:, :half] / sums[0][:, half:],
                sums[1][:, half:] / sums[1][:, :half],
            ],
            axis=1,
        ).astype(BF)
        return seqs[t].astype(F32) + mm(attended, wo[which])

    def feed_forward(q):
        pltpu.make_async_copy(home3.at[q], home3.at[q], b_recv.at[q]).wait()
        for b in range(0, length, 256):
            y = home3[q, b : b + 256, :].astype(F32)
            hidden = jax.nn.gelu(mm(rms(y).astype(BF), up[...]), approximate=True)
            res[q, b : b + 256, :] = (y + mm(hidden.astype(BF), down[...])).astype(BF)

    def out_copy(m, b):
        rows = pl.ds(b * 16, 16)
        return pltpu.make_async_copy(out_v.at[m, rows], out_ref.at[m, rows], o_sem.at[m, b])

    def finish(m):
        for b in range(4):
            parts = [
                res[2 * m + j, n * 64 + b * 16 : n * 64 + b * 16 + 16, :]
                for j in range(2)
                for n in range(8)
            ]
            moved = mm(perm_a[...], jnp.concatenate(parts, axis=0))
            out_v[m, b * 16 : (b + 1) * 16] = moved.reshape(16, 16, width).astype(BF)
            out_copy(m, b).start()

    for copy in weight_copies:
        copy.wait()

    def step(t, _):
        @pl.when(t < 4)
        def _():
            pltpu.make_async_copy(seqs.at[t], seqs.at[t], in_recv.at[t & 3]).wait()

        @pl.when(t >= 4)
        def _():
            pltpu.make_async_copy(seqs.at[t], seqs.at[t], c_recv.at[t & 3]).wait()

        done = attention(t)

        @pl.when(t < 4)
        def _():
            rowres[t & 1] = done.astype(BF)

        @pl.when(t >= 4)
        def _():
            pieces = [
                done[n * 64 + p * 8 : n * 64 + p * 8 + 8, :] for p in range(nr) for n in range(nz)
            ]
            colout[t - 4] = jnp.concatenate(pieces, axis=0).astype(BF)
            send_home(t - 4)

        @pl.when(t == 1)
        def _():
            split(0)
            across(0)

        @pl.when(t == 2)
        def _():
            across(1)
            forward(0)

        @pl.when(t == 3)
        def _():
            split(1)
            across(2)
            across(3)
            forward(1)
            forward(2)

        @pl.when(t == 4)
        def _():
            forward(3)

        @pl.when(t == 5)
        def _():
            feed_forward(0)

        return 0

    lax.fori_loop(0, 8, step, 0)
    feed_forward(1)
    finish(0)
    feed_forward(2)
    feed_forward(3)
    finish(1)

    def drain(q, _):
        for ref, sem, rows in (
            (seqs, in_send, (nc - 1) * 16),
            (seqs, p_send, (4 * nr - 1) * 16),
            (seqs, c_send, (nz - 1) * 64),
            (home3, b_send, (nr - 1) * 64),
        ):
            view = ref.at[q, pl.ds(0, rows)]
            pltpu.make_async_copy(view, view, sem.at[q]).wait()
        return 0

    lax.fori_loop(0, 4, drain, 0)
    for m in range(2):
        for b in range(4):
            out_copy(m, b).wait()


def solution(mesh):
    nr, nc = mesh.shape["row"], mesh.shape["col"]

    def body(cells, *weights):
        width = cells.shape[-1]
        ff = weights[4].shape[1]
        dma4 = pltpu.SemaphoreType.DMA((4,))
        return pl.pallas_call(
            functools.partial(kernel, nr, nc, nc // 4),
            out_shape=jax.ShapeDtypeStruct(cells.shape, BF),
            in_specs=[pl.BlockSpec(memory_space=pl.ANY)] * 7,
            out_specs=pl.BlockSpec(memory_space=pl.ANY),
            scratch_shapes=[
                pltpu.VMEM((2, width, 3 * width), BF),
                pltpu.VMEM((2, width, width), BF),
                pltpu.VMEM((width, ff), BF),
                pltpu.VMEM((ff, width), BF),
                pltpu.VMEM((8, 512, width), BF),
                pltpu.VMEM((2, 512, width), BF),
                pltpu.VMEM((4, 4 * nr, 16, width), BF),
                pltpu.VMEM((4, 512, width), BF),
                pltpu.VMEM((4, nc // 4, 64, width), BF),
                pltpu.VMEM((4, 512, width), BF),
                pltpu.VMEM((4, 512, width), BF),
                pltpu.VMEM((4, 512, width), BF),
                pltpu.VMEM((512, width), BF),
                pltpu.VMEM((512, width), BF),
                pltpu.VMEM((HEADS * 512, width), BF),
                pltpu.VMEM((256, 256), BF),
                pltpu.VMEM((256, 256), BF),
                pltpu.VMEM(cells.shape, BF),
                pltpu.SemaphoreType.DMA((6,)),
                pltpu.SemaphoreType.DMA((2, 4)),
            ]
            + [dma4] * 8,
            compiler_params=pltpu.CompilerParams(
                collective_id=0, has_side_effects=True, vmem_limit_bytes=56 << 20
            ),
            name="axial",
        )(cells, *weights)

    return jax.shard_map(
        body,
        mesh=mesh,
        in_specs=(P(None, "row", "col", None),) + (P(),) * 6,
        out_specs=P(None, "row", "col", None),
        check_vma=False,
    )
```
